512 devices in a mesh: dp: 32 (over y, z_hi, core), hidden: 16 (over x, z_lo).
Axes of the slice: x: 4, y: 4, z: 16 (z_hi: 4, z_lo: 4; z = z_hi * 4 + z_lo), core: 2. Of those that a mesh axis runs over, the one named last changes fastest.
Arguments:
- grad_out: bfloat16 [4096, 8192], P('dp', 'hidden'), may hold values from -6 to 6
- signs: int32 [8192], P('hidden'), may hold values from 0 to 1
- weight: bfloat16 [16384, 8192], P('dp', 'hidden'), may hold values from -0.046875 to 0.046875
- activations: bfloat16 [4096, 16384], P('hidden', 'dp'), may hold values from -15 to 15
- outliers: int32 [128], replicated, may hold values from 0 to 16383
Outputs:
- input_grad: bfloat16 [4096, 16384], P('hidden', 'dp')
- weight_grad: float32 [16384, 8192], P('dp', 'hidden')
The draws below stay inside these ranges and needn't reach their ends.
Inputs may be any that keep to these rules, and one draw needn't show every extreme that they name: `outliers`: entries may repeat.
All inputs are finite; a program needn't handle non-finite values.
Results may differ from the reference program's by a relative error of at most 0.023.
Values may be sent and summed in bfloat16 or wider, within the bound.
No kernel may reach another device: no remote copies, remote signals or barrier semaphores. Data moves between devices by JAX's collectives and lax.ppermute only.
A program may use at most 64 MiB of HBM per device.

```python
import math
import jax
import jax.numpy as jnp
from jax import lax

D = 8192
FF = 16384
OUTLIERS = 128
TOKENS = 4096
N_HIDDEN = 16


def set_ends(drawn, own_key, smallest, largest):
    place = [jax.random.randint(jax.random.fold_in(own_key, axis), (), 0, length) for axis, length in enumerate(drawn.shape)]
    widest = drawn.shape.index(max(drawn.shape))
    beside = place[:widest] + [(place[widest] + 1) % drawn.shape[widest]] + place[widest + 1:]
    return drawn.at[tuple(place)].set(smallest).at[tuple(beside)].set(largest)


def levels(rng, shape, shards, smallest, top_value):
    def one(dim, parts):
        heights = jax.random.uniform(jax.random.fold_in(jax.random.fold_in(rng, 6), dim), (parts,), jnp.float32, smallest / len(shards), top_value / len(shards))
        return jnp.repeat(jnp.exp(heights), shape[dim] // parts).reshape((-1,) + (1,) * (len(shape) - dim - 1))

    factor_of = one(*shards[0])
    for cut in shards[1:]:
        factor_of = factor_of * one(*cut)
    return factor_of


def bell_draw(own_key, extent, deviation, reach, pieces=(), kind=jnp.bfloat16):
    entries = jax.random.normal(own_key, extent, jnp.float32) * deviation
    if len(pieces) > 0:
        entries = levels(own_key, extent, pieces, -0.22, 0.18) * entries
    return jnp.clip(entries, min=-reach, max=reach).astype(kind)


def setup_inputs(seed: int = 0) -> dict:
    seeds = jax.random.split(jax.random.key(seed), 6)
    grad_out = bell_draw(seeds[0], (TOKENS, D), 1.0, 6.0, ((0, 32), (1, 16)))
    signs = set_ends(jax.random.randint(seeds[1], (D,), 0, 2), jax.random.fold_in(seeds[1], 1), 0, 1).astype(jnp.int32)
    weight = bell_draw(seeds[2], (FF, D), FF ** -0.5, 0.046875, ((0, 32), (1, 16)))
    activations = bell_draw(seeds[3], (TOKENS, FF), 2.5, 15.0, ((0, 16), (1, 32)))
    outliers = set_ends(jax.random.randint(seeds[4], (OUTLIERS,), 0, FF), jax.random.fold_in(seeds[4], 1), 0, FF - 1).astype(jnp.int32)
    return {"grad_out": grad_out, "signs": signs, "weight": weight, "activations": activations, "outliers": outliers}


def hadamard_table(order):
    index = jnp.arange(order, dtype=jnp.int32)
    count = jnp.zeros((order, order), jnp.int32)
    for level in range(order.bit_length() - 1):
        step = 2 ** level
        count = count + index[:, None] // step % 2 * (index[None, :] // step % 2)
    return jnp.where(count % 2 == 0, 1.0, -1.0).astype(jnp.float32)

def reference(grad_out, signs, weight, activations, outliers):
    flips = (2 * signs - 1).astype(jnp.float32)
    signed = grad_out.astype(jnp.float32) * flips[None, :]
    bits = D.bit_length() - 1
    left = 2 ** (bits // 2)
    right = D // left
    shaped = signed.reshape(TOKENS, left, right)
    first = jnp.einsum('tar,rs->tas', shaped, hadamard_table(right), precision=lax.Precision.HIGHEST)
    second = jnp.einsum('ab,tbs->tas', hadamard_table(left), first, precision=lax.Precision.HIGHEST)
    rotated = (second.reshape(TOKENS, D) / math.sqrt(D)).astype(jnp.bfloat16)
    special = jnp.any(jnp.arange(FF, dtype=jnp.int32)[:, None] == outliers[None, :], axis=1)
    clipped = jnp.where(special[None, :], activations, jnp.clip(activations, -3.0, 3.0)).astype(jnp.bfloat16)
    block = D // N_HIDDEN
    summed = jnp.zeros((TOKENS, FF), jnp.float32)
    for part in range(N_HIDDEN):
        piece = jnp.dot(rotated[:, part * block:(part + 1) * block], weight[:, part * block:(part + 1) * block].T, preferred_element_type=jnp.float32)
        rounded = lax.optimization_barrier(piece.astype(jnp.bfloat16))
        summed = summed + rounded.astype(jnp.float32)
    kept = special[None, :] | (jnp.abs(activations.astype(jnp.float32)) <= 3.0)
    input_grad = jnp.where(kept, summed, 0.0).astype(jnp.bfloat16)
    weight_grad = jnp.dot(clipped.T, rotated, preferred_element_type=jnp.float32) / math.sqrt(TOKENS)
    return (input_grad, weight_grad)
```

```python
import math

import jax
import jax.numpy as jnp
from jax import lax
from jax.sharding import Mesh, PartitionSpec as P


def hadamard_table(order):
    index = jnp.arange(order, dtype=jnp.int32)
    count = jnp.zeros((order, order), jnp.int32)
    for level in range(order.bit_length() - 1):
        step = 2**level
        count = count + index[:, None] // step % 2 * (index[None, :] // step % 2)
    return jnp.where(count % 2 == 0, 1.0, -1.0).astype(jnp.float32)


def rotate_rows(rows, width):
    groups = rows.shape[0] // 8
    local = jnp.dot(
        rows, hadamard_table(width).astype(jnp.bfloat16), preferred_element_type=jnp.float32
    )
    local = local.reshape(groups, 8, width)
    step = 1
    while step < groups:
        pairs = local.reshape(groups // (2 * step), 2, step, 8, width)
        low, high = pairs[:, 0], pairs[:, 1]
        local = jnp.stack([low + high, low - high], axis=1).reshape(groups, 8, width)
        step *= 2
    return local


def on_device(grad_out, signs, weight, activations, outliers):
    n_y, n_zh, n_x, n_zl = (lax.axis_size(a) for a in ("y", "zh", "x", "zl"))
    hidden = n_x * n_zl
    tok, width = grad_out.shape
    act_rows, ff = activations.shape
    per = tok // hidden
    quarter = tok // n_x
    total = width * hidden
    factor = 1.0 / math.sqrt(total)
    token_scale = 1.0 / math.sqrt(tok * n_y * n_zh * 2)
    core = lax.axis_index("c")

    weights = lax.all_gather(weight, "x", axis=1, tiled=True)

    flips = (2 * signs - 1).astype(jnp.bfloat16)
    signed = grad_out * flips[None, :]
    rows = lax.all_to_all(signed, ("x", "zl"), split_axis=0, concat_axis=0, tiled=True)
    rotated = (rotate_rows(rows, width) * factor).astype(jnp.bfloat16)
    pieces = rotated.reshape(n_x, n_zl, per, width).transpose(1, 2, 0, 3)
    pieces = pieces.reshape(n_zl, per, n_x * width)
    spread = jnp.broadcast_to(pieces[None], (n_zh, n_zl, per, n_x * width))
    spread = spread.reshape(n_zh * n_zl * per, n_x * width)
    mine = lax.all_to_all(spread, ("zh", "zl"), split_axis=0, concat_axis=0, tiled=True)
    own = lax.all_gather(mine, "y", axis=0, tiled=True)
    other = lax.ppermute(own, "c", [(0, 1), (1, 0)])

    channel = (
        (lax.axis_index("y") * n_zh + lax.axis_index("zh")) * 2 + core
    ) * ff + jnp.arange(ff, dtype=jnp.int32)
    special = jnp.any(channel[:, None] == outliers[None, :], axis=1)
    clipped = jnp.where(special[None, :], activations, jnp.clip(activations, -3.0, 3.0))
    clipped = clipped.reshape(2, n_x, quarter, ff).transpose(1, 0, 2, 3)
    clipped = clipped.reshape(n_x * 2 * quarter, ff)
    swapped = lax.all_to_all(clipped, "x", split_axis=0, concat_axis=0, tiled=True)
    acts = lax.all_gather(swapped, "zl", axis=0, tiled=True)
    acts = acts.reshape(n_zl, n_x, 2, quarter, ff).transpose(2, 1, 0, 3, 4)
    acts = acts.reshape(2, hidden * quarter, ff)
    acts_own = jnp.where(core == 0, acts[0], acts[1])
    acts_other = jnp.where(core == 0, acts[1], acts[0])

    def product(a, b, dims):
        return lax.dot_general(a, b, (dims, ((), ())), preferred_element_type=jnp.float32)

    wg = product(acts_own, own, ((0,), (0,))) + product(acts_other, other, ((0,), (0,)))
    wg = (wg * token_scale).astype(jnp.bfloat16).reshape(ff, n_x, width).transpose(1, 0, 2)
    wg = lax.psum_scatter(wg, "x", scatter_dimension=0, tiled=True)
    weight_grad = wg.reshape(ff, width).astype(jnp.float32)

    parts = [
        product(half, weights, ((1,), (1,))).astype(jnp.bfloat16).reshape(hidden, 1, quarter, ff)
        for half in (own, other)
    ]
    parts = jnp.concatenate(parts, axis=1).reshape(hidden * 2 * quarter, ff)
    parts = lax.all_to_all(parts, ("x", "zl"), split_axis=0, concat_axis=0, tiled=True)
    parts = parts.reshape(n_x, n_zl, 2, quarter, ff).astype(jnp.float32)
    summed = jnp.sum(parts, axis=1)
    first = jnp.where(core == 0, summed[:, 0], summed[:, 1])
    second = jnp.where(core == 0, summed[:, 1], summed[:, 0])
    summed = jnp.stack([first, second], axis=0).reshape(act_rows, ff)
    kept = special[None, :] | (jnp.abs(activations.astype(jnp.float32)) <= 3.0)
    input_grad = jnp.where(kept, summed, 0.0).astype(jnp.bfloat16)
    return (input_grad, weight_grad)


def solution(mesh):
    fine = Mesh(mesh.devices.reshape(4, 4, 2, 4, 4), ("y", "zh", "c", "x", "zl"))
    dp, hidden = ("y", "zh", "c"), ("x", "zl")
    in_specs = (P(dp, hidden), P(hidden), P(dp, hidden), P(hidden, dp), P())
    out_specs = (P(hidden, dp), P(dp, hidden))
    return jax.shard_map(
        on_device, mesh=fine, in_specs=in_specs, out_specs=out_specs, check_vma=False
    )
```

```python
import math

import jax
import jax.numpy as jnp
from jax import lax
from jax.sharding import Mesh, PartitionSpec as P


def hadamard_table(order):
    index = jnp.arange(order, dtype=jnp.int32)
    count = jnp.zeros((order, order), jnp.int32)
    for level in range(order.bit_length() - 1):
        step = 2**level
        count = count + index[:, None] // step % 2 * (index[None, :] // step % 2)
    return jnp.where(count % 2 == 0, 1.0, -1.0).astype(jnp.float32)


def rotate_rows(rows, width, n_x, n_zl):
    tokens = rows.shape[0] // (n_x * n_zl)
    local = jnp.dot(
        rows, hadamard_table(width).astype(jnp.bfloat16), preferred_element_type=jnp.float32
    )
    local = local.reshape(n_x, n_zl, tokens, width)
    both = jnp.bitwise_and(lax.axis_index("zl"), jnp.arange(n_zl, dtype=jnp.int32))
    odd = jnp.bitwise_xor(both, both >> 1) & 1
    local = jnp.sum(local * (1 - 2 * odd).astype(jnp.float32)[None, :, None, None], axis=1)
    b0, b1, b2, b3 = (local[i] for i in range(n_x))
    s0, d0, s1, d1 = b0 + b1, b0 - b1, b2 + b3, b2 - b3
    return jnp.concatenate([s0 + s1, d0 + d1, s0 - s1, d0 - d1], axis=1)


def shifted(array, axis, by):
    n = lax.axis_size(axis)
    return lax.ppermute(array, axis, [(i, (i + by) % n) for i in range(n)])


def on_device(grad_out, signs, weight, activations, outliers):
    n_y, n_zh, n_x, n_zl = (lax.axis_size(a) for a in ("y", "zh", "x", "zl"))
    hidden = n_x * n_zl
    tok, width = grad_out.shape
    act_rows, ff = activations.shape
    quarter = tok // n_x
    total = width * hidden
    factor = 1.0 / math.sqrt(total)
    token_scale = 1.0 / math.sqrt(tok * n_y * n_zh * 2)
    core = lax.axis_index("c")

    weights = lax.all_gather(weight, "x", axis=1, tiled=True)

    flips = (2 * signs - 1).astype(jnp.bfloat16)
    signed = grad_out * flips[None, :]
    spread = jnp.broadcast_to(
        signed.reshape(n_x, 1, quarter, width), (n_x, n_zl, quarter, width)
    ).reshape(hidden * quarter, width)
    rows = lax.all_to_all(spread, ("x", "zl"), split_axis=0, concat_axis=0, tiled=True)
    mine = (rotate_rows(rows, width, n_x, n_zl) * factor).astype(jnp.bfloat16)
    y, zh = lax.axis_index("y"), lax.axis_index("zh")
    own = jnp.zeros((n_y, n_zh, quarter, n_x * width), jnp.bfloat16)
    for k in range(n_zh):
        block = shifted(mine, "zh", k) if k else mine
        for j in range(n_y):
            piece = shifted(block, "y", j) if j else block
            place = ((y + n_y - j) % n_y, (zh + n_zh - k) % n_zh, 0, 0)
            own = lax.dynamic_update_slice(own, piece[None, None], place)
    own = own.reshape(hidden * quarter, n_x * width)
    other = lax.ppermute(own, "c", [(0, 1), (1, 0)])

    channel = (
        (lax.axis_index("y") * n_zh + lax.axis_index("zh")) * 2 + core
    ) * ff + jnp.arange(ff, dtype=jnp.int32)
    special = jnp.any(channel[:, None] == outliers[None, :], axis=1)
    clipped = jnp.where(special[None, :], activations, jnp.clip(activations, -3.0, 3.0))
    clipped = clipped.reshape(2, n_x, quarter, ff).transpose(1, 0, 2, 3)
    clipped = clipped.reshape(n_x * 2 * quarter, ff)
    swapped = lax.all_to_all(clipped, "x", split_axis=0, concat_axis=0, tiled=True)
    acts = lax.all_gather(swapped, "zl", axis=0, tiled=True)
    acts = acts.reshape(n_zl, n_x, 2, quarter, ff).transpose(2, 1, 0, 3, 4)
    acts = acts.reshape(2, hidden * quarter, ff)
    acts_own = jnp.where(core == 0, acts[0], acts[1])
    acts_other = jnp.where(core == 0, acts[1], acts[0])

    def product(a, b, dims):
        return lax.dot_general(a, b, (dims, ((), ())), preferred_element_type=jnp.float32)

    wg = product(acts_own, own, ((0,), (0,))) + product(acts_other, other, ((0,), (0,)))
    wg = (wg * token_scale).astype(jnp.bfloat16).reshape(ff, n_x, width).transpose(1, 0, 2)
    wg = lax.psum_scatter(wg, "x", scatter_dimension=0, tiled=True)
    weight_grad = wg.reshape(ff, width).astype(jnp.float32)

    parts = [
        product(half, weights, ((1,), (1,))).astype(jnp.bfloat16).reshape(hidden, 1, quarter, ff)
        for half in (own, other)
    ]
    parts = jnp.concatenate(parts, axis=1).reshape(hidden * 2 * quarter, ff)
    parts = lax.all_to_all(parts, ("x", "zl"), split_axis=0, concat_axis=0, tiled=True)
    parts = parts.reshape(n_x, n_zl, 2, quarter, ff).astype(jnp.float32)
    summed = jnp.sum(parts, axis=1)
    first = jnp.where(core == 0, summed[:, 0], summed[:, 1])
    second = jnp.where(core == 0, summed[:, 1], summed[:, 0])
    summed = jnp.stack([first, second], axis=0).reshape(act_rows, ff)
    kept = special[None, :] | (jnp.abs(activations.astype(jnp.float32)) <= 3.0)
    input_grad = jnp.where(kept, summed, 0.0).astype(jnp.bfloat16)
    return (input_grad, weight_grad)


def solution(mesh):
    fine = Mesh(mesh.devices.reshape(4, 4, 2, 4, 4), ("y", "zh", "c", "x", "zl"))
    dp, hidden = ("y", "zh", "c"), ("x", "zl")
    in_specs = (P(dp, hidden), P(hidden), P(dp, hidden), P(hidden, dp), P())
    out_specs = (P(hidden, dp), P(dp, hidden))
    return jax.shard_map(
        on_device, mesh=fine, in_specs=in_specs, out_specs=out_specs, check_vma=False
    )
```

```python
import math

import jax
import jax.numpy as jnp
from jax import lax
from jax.experimental import pallas as pl
from jax.experimental.pallas import tpu as pltpu
from jax.sharding import Mesh, PartitionSpec as P


def hadamard_table(order):
    index = jnp.arange(order, dtype=jnp.int32)
    count = jnp.zeros((order, order), jnp.int32)
    for level in range(order.bit_length() - 1):
        step = 2**level
        count = count + index[:, None] // step % 2 * (index[None, :] // step % 2)
    return jnp.where(count % 2 == 0, 1.0, -1.0).astype(jnp.float32)


def parity_signs(a, b):
    both = jnp.bitwise_and(a, b)
    return (1 - 2 * (jnp.bitwise_xor(both, both >> 1) & 1)).astype(jnp.float32)


def rotate_rows(rows, width, n_x, n_zl):
    tokens = rows.shape[0] // (n_x * n_zl)
    local = jnp.dot(
        rows, hadamard_table(width).astype(jnp.bfloat16), preferred_element_type=jnp.float32
    )
    local = local.reshape(n_x, n_zl, tokens, width)
    every = jnp.arange(n_zl, dtype=jnp.int32)
    local = jnp.sum(
        local * parity_signs(lax.axis_index("zl"), every)[None, :, None, None], axis=1
    )
    b0, b1, b2, b3 = (local[i] for i in range(n_x))
    s0, d0, s1, d1 = b0 + b1, b0 - b1, b2 + b3, b2 - b3
    return jnp.concatenate([s0 + s1, d0 + d1, s0 - s1, d0 - d1], axis=1)


def shifted(array, axis, by):
    n = lax.axis_size(axis)
    return lax.ppermute(array, axis, [(i, (i + by) % n) for i in range(n)])


def picked(array, index):
    return lax.dynamic_index_in_dim(array, index, 0, keepdims=False)


def exchanged(pieces, axis):
    n = lax.axis_size(axis)
    me = lax.axis_index(axis)
    came = pieces
    for by in range(1, n):
        piece = shifted(picked(pieces, (me + by) % n), axis, by)
        came = lax.dynamic_update_slice_in_dim(came, piece[None], (me + n - by) % n, 0)
    return came


def spread_over(array, axis):
    n = lax.axis_size(axis)
    copies = jnp.broadcast_to(array[None], (n,) + array.shape)
    return lax.all_to_all(copies, axis, split_axis=0, concat_axis=0, tiled=True)


def weight_kernel(scale, core_ref, acts_ref, own_ref, other_ref, out_ref, rows_ref, turned_ref):
    tokens = own_ref.shape[0]
    n_zl, n_x, _, quarter, _ = acts_ref.shape

    @pl.when(pl.program_id(0) == 0)
    def _():
        for half in range(2):
            core = jnp.bitwise_xor(core_ref[0], half)
            for i in range(n_x):
                for j in range(n_zl):
                    at = half * tokens + (i * n_zl + j) * quarter
                    rows_ref[at : at + quarter, :] = acts_ref[j, i, core]
        turned_ref[...] = rows_ref[...].T

    part = jnp.dot(turned_ref[:, :tokens], own_ref[...], preferred_element_type=jnp.float32)
    part += jnp.dot(turned_ref[:, tokens:], other_ref[...], preferred_element_type=jnp.float32)
    out_ref[0] = (part * scale).astype(out_ref.dtype)


def weight_product(core, acts, own, other, width, scale):
    ff = acts.shape[-1]
    tokens, wide = own.shape
    blocks = wide // width
    block = pl.BlockSpec((tokens, width), lambda i: (0, i))
    return pl.pallas_call(
        lambda *refs: weight_kernel(scale, *refs),
        grid=(blocks,),
        in_specs=[
            pl.BlockSpec(memory_space=pltpu.SMEM),
            pl.BlockSpec(acts.shape, lambda i: (0, 0, 0, 0, 0)),
            block,
            block,
        ],
        out_specs=pl.BlockSpec((1, ff, width), lambda i: (i, 0, 0)),
        out_shape=jax.ShapeDtypeStruct((blocks, ff, width), jnp.bfloat16),
        scratch_shapes=[
            pltpu.VMEM((2 * tokens, ff), jnp.bfloat16),
            pltpu.VMEM((ff, 2 * tokens), jnp.bfloat16),
        ],
        compiler_params=pltpu.CompilerParams(vmem_limit_bytes=14 * 2**20),
        cost_estimate=pl.CostEstimate(
            flops=4 * ff * tokens * wide, bytes_accessed=8 * 2**20, transcendentals=0
        ),
        name="weight_product",
    )(core.reshape(1), acts, own, other)


def widen_kernel(in_ref, out_ref):
    out_ref[...] = in_ref[...].astype(out_ref.dtype)


def widen(array):
    rows, width = array.shape
    block = pl.BlockSpec((rows // 2, width), lambda i: (i, 0))
    return pl.pallas_call(
        widen_kernel,
        grid=(2,),
        in_specs=[block],
        out_specs=block,
        out_shape=jax.ShapeDtypeStruct(array.shape, jnp.float32),
        cost_estimate=pl.CostEstimate(flops=6 * 10**10, bytes_accessed=2**22, transcendentals=0),
        name="widen",
    )(array)


def input_kernel(own_ref, other_ref, weight_ref, _, out_ref):
    blocks, ff, width = weight_ref.shape

    def product(rows_ref):
        total = jnp.zeros((rows_ref.shape[0], ff), jnp.float32)
        for i in range(blocks):
            total += lax.dot_general(
                rows_ref[:, i * width : (i + 1) * width],
                weight_ref[i],
                (((1,), (1,)), ((), ())),
                preferred_element_type=jnp.float32,
            )
        out_ref[...] = total.astype(out_ref.dtype).reshape(out_ref.shape)

    @pl.when(pl.program_id(0) == 0)
    def _():
        product(own_ref)

    @pl.when(pl.program_id(0) == 1)
    def _():
        product(other_ref)


def input_product(own, other, weights, after, quarter):
    tokens, wide = own.shape
    ff = weights.shape[1]
    steps = 2
    rows = tokens // steps
    return pl.pallas_call(
        input_kernel,
        grid=(2, steps),
        in_specs=[
            pl.BlockSpec((rows, wide), lambda h, i: (jnp.where(h == 0, i, steps - 1), 0)),
            pl.BlockSpec((rows, wide), lambda h, i: (jnp.where(h == 0, 0, i), 0)),
            pl.BlockSpec(weights.shape, lambda h, i: (0, 0, 0)),
            pl.BlockSpec(memory_space=pl.ANY),
        ],
        out_specs=pl.BlockSpec((rows // quarter, 1, quarter, ff), lambda h, i: (i, h, 0, 0)),
        out_shape=jax.ShapeDtypeStruct((tokens // quarter, 2, quarter, ff), jnp.bfloat16),
        compiler_params=pltpu.CompilerParams(vmem_limit_bytes=14 * 2**20),
        cost_estimate=pl.CostEstimate(
            flops=4 * ff * tokens * wide, bytes_accessed=8 * 2**20, transcendentals=0
        ),
        name="input_product",
    )(own, other, weights, after)


def on_device(grad_out, signs, weight, activations, outliers):
    n_y, n_zh, n_x, n_zl = (lax.axis_size(a) for a in ("y", "zh", "x", "zl"))
    hidden = n_x * n_zl
    tok, width = grad_out.shape
    ff = activations.shape[1]
    quarter = tok // n_x
    wide = n_x * width
    factor = 1.0 / math.sqrt(width * hidden)
    token_scale = 1.0 / math.sqrt(tok * n_y * n_zh * 2)
    y, zh, core, x = (lax.axis_index(a) for a in ("y", "zh", "c", "x"))

    gathered = lax.all_gather(weight, "x", axis=0)

    channel = ((y * n_zh + zh) * 2 + core) * ff + jnp.arange(ff, dtype=jnp.int32)
    special = jnp.any(channel[:, None] == outliers[None, :], axis=1)
    clipped = jnp.where(special[None, :], activations, jnp.clip(activations, -3.0, 3.0))
    acts = exchanged(clipped.reshape(2, n_x, quarter, ff).transpose(1, 0, 2, 3), "x")

    flips = (2 * signs - 1).astype(jnp.bfloat16)
    signed = grad_out * flips[None, :]
    spread = jnp.broadcast_to(
        signed.reshape(n_x, 1, quarter, width), (n_x, n_zl, quarter, width)
    ).reshape(hidden * quarter, width)
    rows = lax.all_to_all(spread, ("x", "zl"), split_axis=0, concat_axis=0, tiled=True)
    mine = (rotate_rows(rows, width, n_x, n_zl) * factor).astype(jnp.bfloat16)
    mine, acts = lax.optimization_barrier((mine, acts))
    acts = lax.all_gather(acts, "zl", axis=0)

    own = jnp.zeros((n_y, n_zh, quarter, wide), jnp.bfloat16)
    own = lax.dynamic_update_slice(own, spread_over(mine, "y")[:, None], (0, zh, 0, 0))
    along = lax.all_gather(mine, "zh", axis=0)
    along, own, gathered = lax.optimization_barrier((along, own, gathered))
    one, two, three = (picked(along, (zh + r) % n_zh) for r in range(1, n_zh))
    half = quarter // 2
    left = spread_over(jnp.concatenate([two[half:], three], axis=0), "y")
    right = lax.all_gather(jnp.concatenate([one, two[:half]], axis=0), "y", axis=0)
    for block, r, low in (
        (right[:, :quarter], 1, 0),
        (right[:, quarter:], 2, 0),
        (left[:, :half], 2, half),
        (left[:, half:], 3, 0),
    ):
        own = lax.dynamic_update_slice(own, block[:, None], (0, (zh + r) % n_zh, low, 0))
    own = own.reshape(hidden * quarter, wide)
    own, acts = lax.optimization_barrier((own, acts))
    other = lax.ppermute(own, "c", [(0, 1), (1, 0)])

    parts = weight_product(core, acts, own, other, width, token_scale)
    weight_grad = widen(lax.psum_scatter(parts, "x", scatter_dimension=0))

    part = input_product(own, other, gathered, parts, quarter)
    part = lax.all_to_all(part, ("x", "zl"), split_axis=0, concat_axis=0, tiled=True)
    part, weight_grad = lax.optimization_barrier((part, weight_grad))
    part = part.reshape(n_x, n_zl, 2, quarter, ff).astype(jnp.float32)
    summed = jnp.sum(part, axis=1)
    first = jnp.where(core == 0, summed[:, 0], summed[:, 1])
    second = jnp.where(core == 0, summed[:, 1], summed[:, 0])
    summed = jnp.stack([first, second], axis=0).reshape(activations.shape)
    kept = special[None, :] | (jnp.abs(activations.astype(jnp.float32)) <= 3.0)
    input_grad = jnp.where(kept, summed, 0.0).astype(jnp.bfloat16)
    return (input_grad, weight_grad)


def solution(mesh):
    fine = Mesh(mesh.devices.reshape(4, 4, 2, 4, 4), ("y", "zh", "c", "x", "zl"))
    dp, hidden = ("y", "zh", "c"), ("x", "zl")
    in_specs = (P(dp, hidden), P(hidden), P(dp, hidden), P(hidden, dp), P())
    out_specs = (P(hidden, dp), P(dp, hidden))
    return jax.shard_map(
        on_device, mesh=fine, in_specs=in_specs, out_specs=out_specs, check_vma=False
    )
```

```python
import math

import jax
import jax.numpy as jnp
from jax import lax
from jax.experimental import pallas as pl
from jax.experimental.pallas import tpu as pltpu
from jax.sharding import Mesh, PartitionSpec as P


def hadamard_table(order):
    index = jnp.arange(order, dtype=jnp.int32)
    count = jnp.zeros((order, order), jnp.int32)
    for level in range(order.bit_length() - 1):
        step = 2**level
        count = count + index[:, None] // step % 2 * (index[None, :] // step % 2)
    return jnp.where(count % 2 == 0, 1.0, -1.0).astype(jnp.float32)


def parity_signs(a, b):
    both = jnp.bitwise_and(a, b)
    return (1 - 2 * (jnp.bitwise_xor(both, both >> 1) & 1)).astype(jnp.float32)


def rotate_rows(rows, width, n_x, n_zl):
    tokens = rows.shape[0] // (n_x * n_zl)
    local = jnp.dot(
        rows, hadamard_table(width).astype(jnp.bfloat16), preferred_element_type=jnp.float32
    )
    local = local.reshape(n_x, n_zl, tokens, width)
    every = jnp.arange(n_zl, dtype=jnp.int32)
    local = jnp.sum(
        local * parity_signs(lax.axis_index("zl"), every)[None, :, None, None], axis=1
    )
    b0, b1, b2, b3 = (local[i] for i in range(n_x))
    s0, d0, s1, d1 = b0 + b1, b0 - b1, b2 + b3, b2 - b3
    return jnp.concatenate([s0 + s1, d0 + d1, s0 - s1, d0 - d1], axis=1)


def signed_kernel(signs_ref, rows_ref, out_ref):
    n_x, n_zl, quarter, _ = out_ref.shape
    flips = (2 * signs_ref[...] - 1).astype(rows_ref.dtype)
    for i in range(n_x):
        rows = rows_ref[i * quarter : (i + 1) * quarter, :] * flips
        for j in range(n_zl):
            out_ref[i, j] = rows


def signed_rows(grad_out, signs, n_x, n_zl):
    tok, width = grad_out.shape
    whole = pl.BlockSpec(memory_space=pltpu.VMEM)
    return pl.pallas_call(
        signed_kernel,
        in_specs=[whole, whole],
        out_specs=whole,
        out_shape=jax.ShapeDtypeStruct((n_x, n_zl, tok // n_x, width), grad_out.dtype),
        cost_estimate=pl.CostEstimate(flops=0, bytes_accessed=2**20, transcendentals=0),
        name="signed_rows",
    )(signs[None, :], grad_out)


def repeat_kernel(rows_ref, out_ref):
    for i in range(out_ref.shape[0]):
        out_ref[i] = rows_ref[...]


def repeated(rows, times):
    whole = pl.BlockSpec(memory_space=pltpu.VMEM)
    return pl.pallas_call(
        repeat_kernel,
        in_specs=[whole],
        out_specs=whole,
        out_shape=jax.ShapeDtypeStruct((times,) + rows.shape, rows.dtype),
        compiler_params=pltpu.CompilerParams(vmem_limit_bytes=16 * 2**20),
        cost_estimate=pl.CostEstimate(flops=0, bytes_accessed=2**21, transcendentals=0),
        name="repeated",
    )(rows)


def shifted(array, axis, by):
    n = lax.axis_size(axis)
    return lax.ppermute(array, axis, [(i, (i + by) % n) for i in range(n)])


def picked(array, index):
    return lax.dynamic_index_in_dim(array, index, 0, keepdims=False)


def exchanged(pieces, axis):
    n = lax.axis_size(axis)
    me = lax.axis_index(axis)
    came = pieces
    for by in range(1, n):
        piece = shifted(picked(pieces, (me + by) % n), axis, by)
        came = lax.dynamic_update_slice_in_dim(came, piece[None], (me + n - by) % n, 0)
    return came


def spread_over(array, axis):
    n = lax.axis_size(axis)
    copies = repeated(array, n)
    return lax.all_to_all(copies, axis, split_axis=0, concat_axis=0, tiled=True)


def turn_kernel(core_ref, acts_ref, out_ref, rows_ref):
    n_zl, n_x, _, quarter, _ = acts_ref.shape
    tokens = n_zl * n_x * quarter
    for half in range(2):
        core = jnp.bitwise_xor(core_ref[0], half)
        for i in range(n_x):
            for j in range(n_zl):
                at = half * tokens + (i * n_zl + j) * quarter
                rows_ref[at : at + quarter, :] = acts_ref[j, i, core]
    out_ref[...] = rows_ref[...].T


def turned(core, acts):
    ff = acts.shape[-1]
    tokens = acts.size // ff
    return pl.pallas_call(
        turn_kernel,
        in_specs=[
            pl.BlockSpec(memory_space=pltpu.SMEM),
            pl.BlockSpec(memory_space=pltpu.VMEM),
        ],
        out_specs=pl.BlockSpec(memory_space=pltpu.VMEM),
        out_shape=jax.ShapeDtypeStruct((ff, tokens), acts.dtype),
        scratch_shapes=[pltpu.VMEM((tokens, ff), acts.dtype)],
        compiler_params=pltpu.CompilerParams(vmem_limit_bytes=16 * 2**20),
        cost_estimate=pl.CostEstimate(flops=6 * 10**10, bytes_accessed=2**21, transcendentals=0),
        name="turned",
    )(core.reshape(1), acts)


def input_part(half, rows_ref, weight_refs, part_ref, out_ref, sends):
    ff, width = weight_refs[0].shape
    groups, quarter, _ = part_ref.shape
    steps = 2
    rows = rows_ref.shape[0] // steps
    out = []
    for j in range(steps):
        total = jnp.zeros((rows, ff), jnp.float32)
        for i, weight_ref in enumerate(weight_refs):
            total += lax.dot_general(
                rows_ref[j * rows : (j + 1) * rows, i * width : (i + 1) * width],
                weight_ref[...],
                (((1,), (1,)), ((), ())),
                preferred_element_type=jnp.float32,
            )
        at = pl.ds(j * (groups // steps), groups // steps)
        part_ref[at] = total.astype(part_ref.dtype).reshape(groups // steps, quarter, ff)
        out.append(pltpu.make_async_copy(part_ref.at[at], out_ref.at[at, half], sends.at[j]))
        out[-1].start()
    return out


def own_kernel(
    acts_ref, rows_ref, weight_ref, weight_part_ref, input_ref, _, held_ref, part_ref, fetches, sends
):
    blocks, _, width = weight_part_ref.shape
    tokens = rows_ref.shape[0]
    fetch = [
        pltpu.make_async_copy(weight_ref.at[i], held_ref.at[i], fetches.at[i])
        for i in range(blocks)
    ]
    for copy in fetch:
        copy.start()
    for i in range(blocks):
        weight_part_ref[i] = jnp.dot(
            acts_ref[:, :tokens],
            rows_ref[:, i * width : (i + 1) * width],
            preferred_element_type=jnp.float32,
        )
    for copy in fetch:
        copy.wait()
    held = [held_ref.at[i] for i in range(blocks)]
    for copy in input_part(0, rows_ref, held, part_ref, input_ref, sends):
        copy.wait()


def other_kernel(
    scale, acts_ref, rows_ref, weight_ref, own_ref, _, __, input_ref, out_ref,
    held_ref, part_ref, weight_part_ref, fetches, sends, weight_sends
):
    blocks, _, width = own_ref.shape
    tokens = rows_ref.shape[0]
    fetch = [
        pltpu.make_async_copy(weight_ref.at[i], held_ref.at[i], fetches.at[i])
        for i in range(blocks)
    ]
    for copy in fetch:
        copy.start()
    out = []
    for i in range(blocks):
        part = own_ref[i] + jnp.dot(
            acts_ref[:, tokens:],
            rows_ref[:, i * width : (i + 1) * width],
            preferred_element_type=jnp.float32,
        )
        weight_part_ref[i] = (part * scale).astype(weight_part_ref.dtype)
        out.append(
            pltpu.make_async_copy(weight_part_ref.at[i], out_ref.at[i], weight_sends.at[i])
        )
        out[-1].start()
    for copy in fetch:
        copy.wait()
    held = [held_ref.at[i] for i in range(blocks)]
    out += input_part(1, rows_ref, held, part_ref, input_ref, sends)
    for copy in out:
        copy.wait()


def products(acts, own, other, weights, quarter, scale):
    blocks, ff, width = weights.shape
    tokens, wide = own.shape
    groups = tokens // quarter
    whole = pl.BlockSpec(memory_space=pltpu.VMEM)
    hbm = pl.BlockSpec(memory_space=pltpu.HBM)
    estimate = pl.CostEstimate(
        flops=4 * ff * tokens * wide, bytes_accessed=8 * 2**20, transcendentals=0
    )
    params = pltpu.CompilerParams(vmem_limit_bytes=20 * 2**20)
    input_shape = jax.ShapeDtypeStruct((groups, 2, quarter, ff), jnp.bfloat16)
    weight_shape = jax.ShapeDtypeStruct(weights.shape, jnp.bfloat16)
    scratch = [
        pltpu.VMEM(weights.shape, weights.dtype),
        pltpu.VMEM((groups, quarter, ff), jnp.bfloat16),
    ]
    sems = [pltpu.SemaphoreType.DMA((blocks,)), pltpu.SemaphoreType.DMA((2,))]
    first, input_part, weight_part = pl.pallas_call(
        own_kernel,
        in_specs=[whole, whole, hbm],
        out_specs=[whole, hbm, hbm],
        out_shape=[
            jax.ShapeDtypeStruct(weights.shape, jnp.float32),
            input_shape,
            weight_shape,
        ],
        scratch_shapes=scratch + sems,
        compiler_params=params,
        cost_estimate=estimate,
        name="products_own",
    )(acts, own, weights)
    input_part, weight_part = pl.pallas_call(
        lambda *refs: other_kernel(scale, *refs),
        in_specs=[whole, whole, hbm, whole, hbm, hbm],
        out_specs=[hbm, hbm],
        out_shape=[input_shape, weight_shape],
        input_output_aliases={4: 0, 5: 1},
        scratch_shapes=scratch
        + [pltpu.VMEM(weights.shape, jnp.bfloat16)]
        + sems
        + [pltpu.SemaphoreType.DMA((blocks,))],
        compiler_params=params,
        cost_estimate=estimate,
        name="products_other",
    )(acts, other, weights, first, input_part, weight_part)
    return weight_part, input_part


def widen_kernel(in_ref, out_ref):
    out_ref[...] = in_ref[...].astype(out_ref.dtype)


def widen(array):
    rows, width = array.shape
    block = pl.BlockSpec((rows // 2, width), lambda i: (i, 0))
    return pl.pallas_call(
        widen_kernel,
        grid=(2,),
        in_specs=[block],
        out_specs=block,
        out_shape=jax.ShapeDtypeStruct(array.shape, jnp.float32),
        cost_estimate=pl.CostEstimate(flops=6 * 10**10, bytes_accessed=2**22, transcendentals=0),
        name="widen",
    )(array)


def on_device(grad_out, signs, weight, activations, outliers):
    n_y, n_zh, n_x, n_zl = (lax.axis_size(a) for a in ("y", "zh", "x", "zl"))
    hidden = n_x * n_zl
    tok, width = grad_out.shape
    ff = activations.shape[1]
    quarter = tok // n_x
    wide = n_x * width
    factor = 1.0 / math.sqrt(width * hidden)
    token_scale = 1.0 / math.sqrt(tok * n_y * n_zh * 2)
    y, zh, core, x = (lax.axis_index(a) for a in ("y", "zh", "c", "x"))

    gathered = lax.all_gather(weight, "x", axis=0)

    channel = ((y * n_zh + zh) * 2 + core) * ff + jnp.arange(ff, dtype=jnp.int32)
    special = jnp.any(channel[:, None] == outliers[None, :], axis=1)
    clipped = jnp.where(special[None, :], activations, jnp.clip(activations, -3.0, 3.0))
    acts = exchanged(clipped.reshape(2, n_x, quarter, ff).transpose(1, 0, 2, 3), "x")

    spread = signed_rows(grad_out, signs, n_x, n_zl).reshape(hidden * quarter, width)
    rows = lax.all_to_all(spread, ("x", "zl"), split_axis=0, concat_axis=0, tiled=True)
    mine = (rotate_rows(rows, width, n_x, n_zl) * factor).astype(jnp.bfloat16)
    mine, acts = lax.optimization_barrier((mine, acts))
    acts = lax.all_gather(acts, "zl", axis=0)

    along = lax.all_gather(mine, "zh", axis=0)
    along, gathered = lax.optimization_barrier((along, gathered))
    own = spread_over(along.reshape(-1, wide), "y").reshape(-1, wide)
    own, acts = lax.optimization_barrier((own, turned(core, acts)))
    other = lax.ppermute(own, "c", [(0, 1), (1, 0)])

    parts, part = products(acts, own, other, gathered, quarter, token_scale)
    weight_grad = widen(lax.psum_scatter(parts, "x", scatter_dimension=0))
    part = lax.all_to_all(part, ("x", "zl"), split_axis=0, concat_axis=0, tiled=True)
    part, weight_grad = lax.optimization_barrier((part, weight_grad))
    part = part.reshape(n_x, n_zl, 2, quarter, ff).astype(jnp.float32)
    summed = jnp.sum(part, axis=1)
    first = jnp.where(core == 0, summed[:, 0], summed[:, 1])
    second = jnp.where(core == 0, summed[:, 1], summed[:, 0])
    summed = jnp.stack([first, second], axis=0).reshape(activations.shape)
    kept = special[None, :] | (jnp.abs(activations.astype(jnp.float32)) <= 3.0)
    input_grad = jnp.where(kept, summed, 0.0).astype(jnp.bfloat16)
    return (input_grad, weight_grad)


def solution(mesh):
    fine = Mesh(mesh.devices.reshape(4, 4, 2, 4, 4), ("y", "zh", "c", "x", "zl"))
    dp, hidden = ("y", "zh", "c"), ("x", "zl")
    in_specs = (P(dp, hidden), P(hidden), P(dp, hidden), P(hidden, dp), P())
    out_specs = (P(hidden, dp), P(dp, hidden))
    return jax.shard_map(
        on_device, mesh=fine, in_specs=in_specs, out_specs=out_specs, check_vma=False
    )
```

```python
import math

import jax
import jax.numpy as jnp
from jax import lax
from jax.experimental import pallas as pl
from jax.experimental.pallas import tpu as pltpu
from jax.sharding import Mesh, PartitionSpec as P


def hadamard_table(order):
    index = jnp.arange(order, dtype=jnp.int32)
    count = jnp.zeros((order, order), jnp.int32)
    for level in range(order.bit_length() - 1):
        step = 2**level
        count = count + index[:, None] // step % 2 * (index[None, :] // step % 2)
    return jnp.where(count % 2 == 0, 1.0, -1.0).astype(jnp.float32)


def parity_signs(a, b):
    both = jnp.bitwise_and(a, b)
    return (1 - 2 * (jnp.bitwise_xor(both, both >> 1) & 1)).astype(jnp.float32)


def rotate_rows(rows, width, n_x, n_zl):
    tokens = rows.shape[0] // (n_x * n_zl)
    local = jnp.dot(
        rows, hadamard_table(width).astype(jnp.bfloat16), preferred_element_type=jnp.float32
    )
    local = local.reshape(n_x, n_zl, tokens, width)
    every = jnp.arange(n_zl, dtype=jnp.int32)
    local = jnp.sum(
        local * parity_signs(lax.axis_index("zl"), every)[None, :, None, None], axis=1
    )
    b0, b1, b2, b3 = (local[i] for i in range(n_x))
    s0, d0, s1, d1 = b0 + b1, b0 - b1, b2 + b3, b2 - b3
    return jnp.concatenate([s0 + s1, d0 + d1, s0 - s1, d0 - d1], axis=1)


def signed_kernel(signs_ref, rows_ref, out_ref):
    n_x, n_zl, quarter, _ = out_ref.shape
    flips = (2 * signs_ref[...] - 1).astype(rows_ref.dtype)
    for i in range(n_x):
        rows = rows_ref[i * quarter : (i + 1) * quarter, :] * flips
        for j in range(n_zl):
            out_ref[i, j] = rows


def signed_rows(grad_out, signs, n_x, n_zl):
    tok, width = grad_out.shape
    whole = pl.BlockSpec(memory_space=pltpu.VMEM)
    return pl.pallas_call(
        signed_kernel,
        in_specs=[whole, whole],
        out_specs=whole,
        out_shape=jax.ShapeDtypeStruct((n_x, n_zl, tok // n_x, width), grad_out.dtype),
        cost_estimate=pl.CostEstimate(flops=0, bytes_accessed=2**20, transcendentals=0),
        name="signed_rows",
    )(signs[None, :], grad_out)


def repeat_kernel(rows_ref, out_ref):
    for i in range(out_ref.shape[0]):
        out_ref[i] = rows_ref[...]


def repeated(rows, times):
    whole = pl.BlockSpec(memory_space=pltpu.VMEM)
    return pl.pallas_call(
        repeat_kernel,
        in_specs=[whole],
        out_specs=whole,
        out_shape=jax.ShapeDtypeStruct((times,) + rows.shape, rows.dtype),
        compiler_params=pltpu.CompilerParams(vmem_limit_bytes=16 * 2**20),
        cost_estimate=pl.CostEstimate(flops=0, bytes_accessed=2**21, transcendentals=0),
        name="repeated",
    )(rows)


def shifted(array, axis, by):
    n = lax.axis_size(axis)
    return lax.ppermute(array, axis, [(i, (i + by) % n) for i in range(n)])


def picked(array, index):
    return lax.dynamic_index_in_dim(array, index, 0, keepdims=False)


def exchanged(pieces, axis):
    n = lax.axis_size(axis)
    me = lax.axis_index(axis)
    came = pieces
    for by in range(1, n):
        piece = shifted(picked(pieces, (me + by) % n), axis, by)
        came = lax.dynamic_update_slice_in_dim(came, piece[None], (me + n - by) % n, 0)
    return came


def spread_over(array, axis):
    n = lax.axis_size(axis)
    copies = repeated(array, n)
    return lax.all_to_all(copies, axis, split_axis=0, concat_axis=0, tiled=True)


def turn_kernel(core_ref, acts_ref, out_ref, rows_ref):
    n_zl, n_x, _, quarter, _ = acts_ref.shape
    tokens = n_zl * n_x * quarter
    for half in range(2):
        core = jnp.bitwise_xor(core_ref[0], half)
        for i in range(n_x):
            for j in range(n_zl):
                at = half * tokens + (i * n_zl + j) * quarter
                rows_ref[at : at + quarter, :] = acts_ref[j, i, core]
    out_ref[...] = rows_ref[...].T


def turned(core, acts):
    ff = acts.shape[-1]
    tokens = acts.size // ff
    return pl.pallas_call(
        turn_kernel,
        in_specs=[
            pl.BlockSpec(memory_space=pltpu.SMEM),
            pl.BlockSpec(memory_space=pltpu.VMEM),
        ],
        out_specs=pl.BlockSpec(memory_space=pltpu.VMEM),
        out_shape=jax.ShapeDtypeStruct((ff, tokens), acts.dtype),
        scratch_shapes=[pltpu.VMEM((tokens, ff), acts.dtype)],
        compiler_params=pltpu.CompilerParams(vmem_limit_bytes=16 * 2**20),
        cost_estimate=pl.CostEstimate(flops=6 * 10**10, bytes_accessed=2**21, transcendentals=0),
        name="turned",
    )(core.reshape(1), acts)


def input_part(half, rows_ref, weight_refs, part_ref, out_ref, sends):
    ff, width = weight_refs[0].shape
    n_zl, n_x, quarter, _ = part_ref.shape
    steps = 2
    rows = rows_ref.shape[0] // steps
    out = []
    for j in range(steps):
        total = jnp.zeros((rows, ff), jnp.float32)
        for i, weight_ref in enumerate(weight_refs):
            total += lax.dot_general(
                rows_ref[j * rows : (j + 1) * rows, i * width : (i + 1) * width],
                weight_ref[...],
                (((1,), (1,)), ((), ())),
                preferred_element_type=jnp.float32,
            )
        total = total.astype(part_ref.dtype)
        each = n_x // steps
        for group in range(each * n_zl):
            part_ref[group % n_zl, j * each + group // n_zl] = total[
                group * quarter : (group + 1) * quarter
            ]
        at = pl.ds(j * each, each)
        out.append(
            pltpu.make_async_copy(part_ref.at[:, at], out_ref.at[:, at, half], sends.at[j])
        )
        out[-1].start()
    return out


def own_kernel(
    acts_ref, rows_ref, weight_ref, weight_part_ref, input_ref, _, held_ref, part_ref, fetches, sends
):
    blocks, _, width = weight_part_ref.shape
    tokens = rows_ref.shape[0]
    fetch = [
        pltpu.make_async_copy(weight_ref.at[i], held_ref.at[i], fetches.at[i])
        for i in range(blocks)
    ]
    for copy in fetch:
        copy.start()
    for i in range(blocks):
        weight_part_ref[i] = jnp.dot(
            acts_ref[:, :tokens],
            rows_ref[:, i * width : (i + 1) * width],
            preferred_element_type=jnp.float32,
        )
    for copy in fetch:
        copy.wait()
    held = [held_ref.at[i] for i in range(blocks)]
    for copy in input_part(0, rows_ref, held, part_ref, input_ref, sends):
        copy.wait()


def other_kernel(
    scale, acts_ref, rows_ref, weight_ref, own_ref, _, __, input_ref, out_ref,
    held_ref, part_ref, weight_part_ref, fetches, sends, weight_sends
):
    blocks, _, width = own_ref.shape
    tokens = rows_ref.shape[0]
    fetch = [
        pltpu.make_async_copy(weight_ref.at[i], held_ref.at[i], fetches.at[i])
        for i in range(blocks)
    ]
    for copy in fetch:
        copy.start()
    out = []
    for i in range(blocks):
        part = own_ref[i] + jnp.dot(
            acts_ref[:, tokens:],
            rows_ref[:, i * width : (i + 1) * width],
            preferred_element_type=jnp.float32,
        )
        weight_part_ref[i] = (part * scale).astype(weight_part_ref.dtype)
        out.append(
            pltpu.make_async_copy(weight_part_ref.at[i], out_ref.at[i], weight_sends.at[i])
        )
        out[-1].start()
    for copy in fetch:
        copy.wait()
    held = [held_ref.at[i] for i in range(blocks)]
    out += input_part(1, rows_ref, held, part_ref, input_ref, sends)
    for copy in out:
        copy.wait()


def products(acts, own, other, weights, quarter, scale):
    blocks, ff, width = weights.shape
    tokens, wide = own.shape
    n_zl = tokens // quarter // blocks
    whole = pl.BlockSpec(memory_space=pltpu.VMEM)
    hbm = pl.BlockSpec(memory_space=pltpu.HBM)
    estimate = pl.CostEstimate(
        flops=4 * ff * tokens * wide, bytes_accessed=8 * 2**20, transcendentals=0
    )
    params = pltpu.CompilerParams(vmem_limit_bytes=20 * 2**20)
    input_shape = jax.ShapeDtypeStruct((n_zl, blocks, 2, quarter, ff), jnp.bfloat16)
    weight_shape = jax.ShapeDtypeStruct(weights.shape, jnp.bfloat16)
    scratch = [
        pltpu.VMEM(weights.shape, weights.dtype),
        pltpu.VMEM((n_zl, blocks, quarter, ff), jnp.bfloat16),
    ]
    sems = [pltpu.SemaphoreType.DMA((blocks,)), pltpu.SemaphoreType.DMA((2,))]
    first, input_part, weight_part = pl.pallas_call(
        own_kernel,
        in_specs=[whole, whole, hbm],
        out_specs=[whole, hbm, hbm],
        out_shape=[
            jax.ShapeDtypeStruct(weights.shape, jnp.float32),
            input_shape,
            weight_shape,
        ],
        scratch_shapes=scratch + sems,
        compiler_params=params,
        cost_estimate=estimate,
        name="products_own",
    )(acts, own, weights)
    input_part, weight_part = pl.pallas_call(
        lambda *refs: other_kernel(scale, *refs),
        in_specs=[whole, whole, hbm, whole, hbm, hbm],
        out_specs=[hbm, hbm],
        out_shape=[input_shape, weight_shape],
        input_output_aliases={4: 0, 5: 1},
        scratch_shapes=scratch
        + [pltpu.VMEM(weights.shape, jnp.bfloat16)]
        + sems
        + [pltpu.SemaphoreType.DMA((blocks,))],
        compiler_params=params,
        cost_estimate=estimate,
        name="products_other",
    )(acts, other, weights, first, input_part, weight_part)
    return weight_part, input_part


def widen_kernel(in_ref, out_ref):
    out_ref[...] = in_ref[...].astype(out_ref.dtype)


def widen(array):
    rows, width = array.shape
    block = pl.BlockSpec((rows // 2, width), lambda i: (i, 0))
    return pl.pallas_call(
        widen_kernel,
        grid=(2,),
        in_specs=[block],
        out_specs=block,
        out_shape=jax.ShapeDtypeStruct(array.shape, jnp.float32),
        cost_estimate=pl.CostEstimate(flops=6 * 10**10, bytes_accessed=2**22, transcendentals=0),
        name="widen",
    )(array)


def on_device(grad_out, signs, weight, activations, outliers):
    n_y, n_zh, n_x, n_zl = (lax.axis_size(a) for a in ("y", "zh", "x", "zl"))
    hidden = n_x * n_zl
    tok, width = grad_out.shape
    ff = activations.shape[1]
    quarter = tok // n_x
    wide = n_x * width
    factor = 1.0 / math.sqrt(width * hidden)
    token_scale = 1.0 / math.sqrt(tok * n_y * n_zh * 2)
    y, zh, core, x = (lax.axis_index(a) for a in ("y", "zh", "c", "x"))

    gathered = lax.all_gather(weight, "x", axis=0)

    channel = ((y * n_zh + zh) * 2 + core) * ff + jnp.arange(ff, dtype=jnp.int32)
    special = jnp.any(channel[:, None] == outliers[None, :], axis=1)
    clipped = jnp.where(special[None, :], activations, jnp.clip(activations, -3.0, 3.0))
    acts = exchanged(clipped.reshape(2, n_x, quarter, ff).transpose(1, 0, 2, 3), "x")

    spread = signed_rows(grad_out, signs, n_x, n_zl).reshape(hidden * quarter, width)
    rows = lax.all_to_all(spread, ("x", "zl"), split_axis=0, concat_axis=0, tiled=True)
    mine = (rotate_rows(rows, width, n_x, n_zl) * factor).astype(jnp.bfloat16)
    mine, acts = lax.optimization_barrier((mine, acts))
    acts = lax.all_gather(acts, "zl", axis=0)

    along = lax.all_gather(mine, "zh", axis=0)
    along, gathered = lax.optimization_barrier((along, gathered))
    own = spread_over(along.reshape(-1, wide), "y").reshape(-1, wide)
    own, acts = lax.optimization_barrier((own, turned(core, acts)))
    other = lax.ppermute(own, "c", [(0, 1), (1, 0)])

    parts, part = products(acts, own, other, gathered, quarter, token_scale)
    weight_grad = widen(lax.psum_scatter(parts, "x", scatter_dimension=0))
    part = lax.all_to_all(part, "zl", split_axis=0, concat_axis=0, tiled=True)
    part = jnp.sum(part.astype(jnp.float32), axis=0).astype(jnp.bfloat16)
    summed = lax.all_to_all(part, "x", split_axis=0, concat_axis=0, tiled=True)
    summed, weight_grad = lax.optimization_barrier((summed, weight_grad))
    first = jnp.where(core == 0, summed[:, 0], summed[:, 1])
    second = jnp.where(core == 0, summed[:, 1], summed[:, 0])
    summed = jnp.stack([first, second], axis=0).reshape(activations.shape)
    kept = special[None, :] | (jnp.abs(activations.astype(jnp.float32)) <= 3.0)
    input_grad = jnp.where(kept, summed, 0).astype(jnp.bfloat16)
    return (input_grad, weight_grad)


def solution(mesh):
    fine = Mesh(mesh.devices.reshape(4, 4, 2, 4, 4), ("y", "zh", "c", "x", "zl"))
    dp, hidden = ("y", "zh", "c"), ("x", "zl")
    in_specs = (P(dp, hidden), P(hidden), P(dp, hidden), P(hidden, dp), P())
    out_specs = (P(hidden, dp), P(dp, hidden))
    return jax.shard_map(
        on_device, mesh=fine, in_specs=in_specs, out_specs=out_specs, check_vma=False
    )
```

```python
import math

import jax
import jax.numpy as jnp
from jax import lax
from jax.experimental import pallas as pl
from jax.experimental.pallas import tpu as pltpu
from jax.sharding import Mesh, PartitionSpec as P


def hadamard_table(order):
    index = jnp.arange(order, dtype=jnp.int32)
    count = jnp.zeros((order, order), jnp.int32)
    for level in range(order.bit_length() - 1):
        step = 2**level
        count = count + index[:, None] // step % 2 * (index[None, :] // step % 2)
    return jnp.where(count % 2 == 0, 1.0, -1.0).astype(jnp.float32)


def parity_signs(a, b):
    both = jnp.bitwise_and(a, b)
    return (1 - 2 * (jnp.bitwise_xor(both, both >> 1) & 1)).astype(jnp.float32)


def rotate_rows(rows, width, n_x, n_zl):
    tokens = rows.shape[0] // (n_x * n_zl)
    local = jnp.dot(
        rows, hadamard_table(width).astype(jnp.bfloat16), preferred_element_type=jnp.float32
    )
    local = local.reshape(n_x, n_zl, tokens, width)
    every = jnp.arange(n_zl, dtype=jnp.int32)
    local = jnp.sum(
        local * parity_signs(lax.axis_index("zl"), every)[None, :, None, None], axis=1
    )
    b0, b1, b2, b3 = (local[i] for i in range(n_x))
    s0, d0, s1, d1 = b0 + b1, b0 - b1, b2 + b3, b2 - b3
    return jnp.concatenate([s0 + s1, d0 + d1, s0 - s1, d0 - d1], axis=1)


def signed_kernel(signs_ref, rows_ref, out_ref):
    n_x, n_zl, quarter, _ = out_ref.shape
    flips = (2 * signs_ref[...] - 1).astype(rows_ref.dtype)
    for i in range(n_x):
        rows = rows_ref[i * quarter : (i + 1) * quarter, :] * flips
        for j in range(n_zl):
            out_ref[i, j] = rows


def signed_rows(grad_out, signs, n_x, n_zl):
    tok, width = grad_out.shape
    whole = pl.BlockSpec(memory_space=pltpu.VMEM)
    return pl.pallas_call(
        signed_kernel,
        in_specs=[whole, whole],
        out_specs=whole,
        out_shape=jax.ShapeDtypeStruct((n_x, n_zl, tok // n_x, width), grad_out.dtype),
        cost_estimate=pl.CostEstimate(flops=0, bytes_accessed=2**20, transcendentals=0),
        name="signed_rows",
    )(signs[None, :], grad_out)


def repeat_kernel(rows_ref, out_ref):
    for i in range(out_ref.shape[0]):
        out_ref[i] = rows_ref[...]


def repeated(rows, times):
    whole = pl.BlockSpec(memory_space=pltpu.VMEM)
    return pl.pallas_call(
        repeat_kernel,
        in_specs=[whole],
        out_specs=whole,
        out_shape=jax.ShapeDtypeStruct((times,) + rows.shape, rows.dtype),
        compiler_params=pltpu.CompilerParams(vmem_limit_bytes=16 * 2**20),
        cost_estimate=pl.CostEstimate(flops=0, bytes_accessed=2**21, transcendentals=0),
        name="repeated",
    )(rows)


def shifted(array, axis, by):
    n = lax.axis_size(axis)
    return lax.ppermute(array, axis, [(i, (i + by) % n) for i in range(n)])


def picked(array, index):
    return lax.dynamic_index_in_dim(array, index, 0, keepdims=False)


def exchanged(pieces, axis):
    n = lax.axis_size(axis)
    me = lax.axis_index(axis)
    came = pieces
    for by in range(1, n):
        piece = shifted(picked(pieces, (me + by) % n), axis, by)
        came = lax.dynamic_update_slice_in_dim(came, piece[None], (me + n - by) % n, 0)
    return came


def spread_over(array, axis):
    n = lax.axis_size(axis)
    copies = repeated(array, n)
    return lax.all_to_all(copies, axis, split_axis=0, concat_axis=0, tiled=True)


def turn_kernel(core_ref, acts_ref, out_ref, rows_ref, sems):
    n_zl, n_x, _, quarter, _ = acts_ref.shape
    tokens = n_zl * n_x * quarter
    copies = []
    for half in range(2):
        core = jnp.bitwise_xor(core_ref[0], half)
        for i in range(n_x):
            for j in range(n_zl):
                at = half * tokens + (i * n_zl + j) * quarter
                copies.append(
                    pltpu.make_async_copy(
                        acts_ref.at[j, i, core], rows_ref.at[pl.ds(at, quarter)], sems.at[len(copies)]
                    )
                )
                copies[-1].start()
    for copy in copies:
        copy.wait()
    out_ref[...] = rows_ref[...].T


def turned(core, acts):
    ff = acts.shape[-1]
    tokens = acts.size // ff
    return pl.pallas_call(
        turn_kernel,
        in_specs=[
            pl.BlockSpec(memory_space=pltpu.SMEM),
            pl.BlockSpec(memory_space=pltpu.HBM),
        ],
        out_specs=pl.BlockSpec(memory_space=pltpu.VMEM),
        out_shape=jax.ShapeDtypeStruct((ff, tokens), acts.dtype),
        scratch_shapes=[
            pltpu.VMEM((tokens, ff), acts.dtype),
            pltpu.SemaphoreType.DMA((acts.shape[0] * acts.shape[1] * 2,)),
        ],
        compiler_params=pltpu.CompilerParams(vmem_limit_bytes=16 * 2**20),
        cost_estimate=pl.CostEstimate(flops=6 * 10**10, bytes_accessed=2**21, transcendentals=0),
        name="turned",
    )(core.reshape(1), acts)


def input_part(half, rows_ref, weight_refs, part_ref, out_ref, sends):
    ff, width = weight_refs[0].shape
    n_zl, n_x, quarter, _ = part_ref.shape
    steps = 2
    rows = rows_ref.shape[0] // steps
    out = []
    for j in range(steps):
        total = jnp.zeros((rows, ff), jnp.float32)
        for i, weight_ref in enumerate(weight_refs):
            total += lax.dot_general(
                rows_ref[j * rows : (j + 1) * rows, i * width : (i + 1) * width],
                weight_ref[...],
                (((1,), (1,)), ((), ())),
                preferred_element_type=jnp.float32,
            )
        total = total.astype(part_ref.dtype)
        each = n_x // steps
        for group in range(each * n_zl):
            part_ref[group % n_zl, j * each + group // n_zl] = total[
                group * quarter : (group + 1) * quarter
            ]
        at = pl.ds(j * each, each)
        out.append(
            pltpu.make_async_copy(part_ref.at[:, at], out_ref.at[:, at, half], sends.at[j])
        )
        out[-1].start()
    return out


def own_kernel(
    acts_ref, rows_ref, weight_ref, weight_part_ref, input_ref, _, held_ref, part_ref, fetches, sends
):
    blocks, _, width = weight_part_ref.shape
    tokens = rows_ref.shape[0]
    fetch = [
        pltpu.make_async_copy(weight_ref.at[i], held_ref.at[i], fetches.at[i])
        for i in range(blocks)
    ]
    for copy in fetch:
        copy.start()
    for i in range(blocks):
        weight_part_ref[i] = jnp.dot(
            acts_ref[:, :tokens],
            rows_ref[:, i * width : (i + 1) * width],
            preferred_element_type=jnp.float32,
        )
    for copy in fetch:
        copy.wait()
    held = [held_ref.at[i] for i in range(blocks)]
    for copy in input_part(0, rows_ref, held, part_ref, input_ref, sends):
        copy.wait()


def other_kernel(
    scale, acts_ref, rows_ref, weight_ref, own_ref, _, __, input_ref, out_ref,
    held_ref, part_ref, weight_part_ref, fetches, sends, weight_sends
):
    blocks, _, width = own_ref.shape
    tokens = rows_ref.shape[0]
    fetch = [
        pltpu.make_async_copy(weight_ref.at[i], held_ref.at[i], fetches.at[i])
        for i in range(blocks)
    ]
    for copy in fetch:
        copy.start()
    out = []
    for i in range(blocks):
        part = own_ref[i] + jnp.dot(
            acts_ref[:, tokens:],
            rows_ref[:, i * width : (i + 1) * width],
            preferred_element_type=jnp.float32,
        )
        weight_part_ref[i] = (part * scale).astype(weight_part_ref.dtype)
        out.append(
            pltpu.make_async_copy(weight_part_ref.at[i], out_ref.at[i], weight_sends.at[i])
        )
        out[-1].start()
    for copy in fetch:
        copy.wait()
    held = [held_ref.at[i] for i in range(blocks)]
    out += input_part(1, rows_ref, held, part_ref, input_ref, sends)
    for copy in out:
        copy.wait()


def products(acts, own, other, weights, quarter, scale):
    blocks, ff, width = weights.shape
    tokens, wide = own.shape
    n_zl = tokens // quarter // blocks
    whole = pl.BlockSpec(memory_space=pltpu.VMEM)
    hbm = pl.BlockSpec(memory_space=pltpu.HBM)
    estimate = pl.CostEstimate(
        flops=4 * ff * tokens * wide, bytes_accessed=8 * 2**20, transcendentals=0
    )
    params = pltpu.CompilerParams(vmem_limit_bytes=20 * 2**20)
    input_shape = jax.ShapeDtypeStruct((n_zl, blocks, 2, quarter, ff), jnp.bfloat16)
    weight_shape = jax.ShapeDtypeStruct(weights.shape, jnp.bfloat16)
    scratch = [
        pltpu.VMEM(weights.shape, weights.dtype),
        pltpu.VMEM((n_zl, blocks, quarter, ff), jnp.bfloat16),
    ]
    sems = [pltpu.SemaphoreType.DMA((blocks,)), pltpu.SemaphoreType.DMA((2,))]
    first, input_part, weight_part = pl.pallas_call(
        own_kernel,
        in_specs=[whole, whole, hbm],
        out_specs=[whole, hbm, hbm],
        out_shape=[
            jax.ShapeDtypeStruct(weights.shape, jnp.float32),
            input_shape,
            weight_shape,
        ],
        scratch_shapes=scratch + sems,
        compiler_params=params,
        cost_estimate=estimate,
        name="products_own",
    )(acts, own, weights)
    input_part, weight_part = pl.pallas_call(
        lambda *refs: other_kernel(scale, *refs),
        in_specs=[whole, whole, hbm, whole, hbm, hbm],
        out_specs=[hbm, hbm],
        out_shape=[input_shape, weight_shape],
        input_output_aliases={4: 0, 5: 1},
        scratch_shapes=scratch
        + [pltpu.VMEM(weights.shape, jnp.bfloat16)]
        + sems
        + [pltpu.SemaphoreType.DMA((blocks,))],
        compiler_params=params,
        cost_estimate=estimate,
        name="products_other",
    )(acts, other, weights, first, input_part, weight_part)
    return weight_part, input_part


def widen_kernel(in_ref, out_ref):
    out_ref[...] = in_ref[...].astype(out_ref.dtype)


def widen(array):
    rows, width = array.shape
    block = pl.BlockSpec((rows // 2, width), lambda i: (i, 0))
    return pl.pallas_call(
        widen_kernel,
        grid=(2,),
        in_specs=[block],
        out_specs=block,
        out_shape=jax.ShapeDtypeStruct(array.shape, jnp.float32),
        cost_estimate=pl.CostEstimate(flops=6 * 10**10, bytes_accessed=2**22, transcendentals=0),
        name="widen",
    )(array)


def on_device(grad_out, signs, weight, activations, outliers):
    n_y, n_zh, n_x, n_zl = (lax.axis_size(a) for a in ("y", "zh", "x", "zl"))
    hidden = n_x * n_zl
    tok, width = grad_out.shape
    ff = activations.shape[1]
    quarter = tok // n_x
    wide = n_x * width
    factor = 1.0 / math.sqrt(width * hidden)
    token_scale = 1.0 / math.sqrt(tok * n_y * n_zh * 2)
    y, zh, core, x = (lax.axis_index(a) for a in ("y", "zh", "c", "x"))

    gathered = lax.all_gather(weight, "x", axis=0)

    channel = ((y * n_zh + zh) * 2 + core) * ff + jnp.arange(ff, dtype=jnp.int32)
    special = jnp.any(channel[:, None] == outliers[None, :], axis=1)
    clipped = jnp.where(special[None, :], activations, jnp.clip(activations, -3.0, 3.0))
    acts = exchanged(clipped.reshape(2, n_x, quarter, ff).transpose(1, 0, 2, 3), "x")

    spread = signed_rows(grad_out, signs, n_x, n_zl).reshape(hidden * quarter, width)
    rows = lax.all_to_all(spread, ("x", "zl"), split_axis=0, concat_axis=0, tiled=True)
    mine = (rotate_rows(rows, width, n_x, n_zl) * factor).astype(jnp.bfloat16)
    mine, acts = lax.optimization_barrier((mine, acts))
    acts = lax.all_gather(acts, "zl", axis=0)

    along = lax.all_gather(mine, "zh", axis=0)
    along, gathered = lax.optimization_barrier((along, gathered))
    own = spread_over(along.reshape(-1, wide), "y").reshape(-1, wide)
    own, acts = lax.optimization_barrier((own, turned(core, acts)))
    other = lax.ppermute(own, "c", [(0, 1), (1, 0)])

    parts, part = products(acts, own, other, gathered, quarter, token_scale)
    weight_grad = widen(lax.psum_scatter(parts, "x", scatter_dimension=0))
    part = lax.all_to_all(part, "zl", split_axis=0, concat_axis=0, tiled=True)
    part = jnp.sum(part.astype(jnp.float32), axis=0).astype(jnp.bfloat16)
    summed = lax.all_to_all(part, "x", split_axis=0, concat_axis=0, tiled=True)
    summed, weight_grad = lax.optimization_barrier((summed, weight_grad))
    first = jnp.where(core == 0, summed[:, 0], summed[:, 1])
    second = jnp.where(core == 0, summed[:, 1], summed[:, 0])
    summed = jnp.stack([first, second], axis=0).reshape(activations.shape)
    kept = special[None, :] | (jnp.abs(activations.astype(jnp.float32)) <= 3.0)
    input_grad = jnp.where(kept, summed, 0).astype(jnp.bfloat16)
    return (input_grad, weight_grad)


def solution(mesh):
    fine = Mesh(mesh.devices.reshape(4, 4, 2, 4, 4), ("y", "zh", "c", "x", "zl"))
    dp, hidden = ("y", "zh", "c"), ("x", "zl")
    in_specs = (P(dp, hidden), P(hidden), P(dp, hidden), P(hidden, dp), P())
    out_specs = (P(hidden, dp), P(dp, hidden))
    return jax.shard_map(
        on_device, mesh=fine, in_specs=in_specs, out_specs=out_specs, check_vma=False
    )
```
